32 devices in a mesh: groups: 2 (over x), shot: 2 (over core), space: 8 (over z, y).
Axes of the slice: x: 2, y: 2, z: 4, core: 2. Of those that a mesh axis runs over, the one named last changes fastest.
Arguments:
- coef: float32 [256, 128, 256], P(('groups', 'space')), parts along dimension 0, may hold values from 0.05 to 0.19
- fwd_prev: float32 [4, 128, 128, 256], P(('groups', 'shot'), 'space'), parts along dimension 0, may hold values from -1.2 to 1.2
- fwd_now: float32 [4, 128, 128, 256], P(('groups', 'shot'), 'space'), parts along dimension 0, may hold values from -1.2 to 1.2
- adj_next: float32 [4, 128, 128, 256], P(('groups', 'shot'), 'space'), parts along dimension 0, may hold values from -1.2 to 1.2
- adj_after: float32 [4, 128, 128, 256], P(('groups', 'shot'), 'space'), parts along dimension 0, may hold values from -1.2 to 1.2
- encode: float32 [4, 64], P(('groups', 'shot')), parts along dimension 0, may hold values from -4 to 4
- wavelet: float32 [20, 64], P('groups'), parts along dimension 0, may hold values from -4 to 4
- shot_cells: int32 [128], P('groups'), parts along dimension 0, may hold values from 0 to 4194303
- rec_cells: int32 [2048], P('groups'), parts along dimension 0, may hold values from 0 to 4194303
- records: float32 [4, 10, 1024], P(('groups', 'shot')), parts along dimension 0, may hold values from -1.2 to 1.2
Outputs:
- gradient: float32 [256, 128, 256], P(('groups', 'space'), 'shot'), parts along dimension 0
The draws below stay inside these ranges and needn't reach their ends.
There are 2 independent parts, one for each index of `groups`. The reference program is written for one: setup_inputs(seed, part) draws one part's arguments, and reference() takes and returns one part's arrays. A program takes and returns all parts, laid end to end along the dimension named above; each array names one. Nothing has to cross between parts.
All inputs are finite; a program needn't handle non-finite values.
Results may differ from the reference program's by a relative error of at most 0.0001.
Values sent between devices are 32-bit elements; how exact they have to be, the bound alone decides.
A program may use at most 128 MiB of HBM per device.

```python
import jax
import jax.numpy as jnp

NY = 128
NZ = 256
STEPS = 10
SHOTS = 64
REC = 1024
NX = 128
SUPERS = 2


def set_ends(result, rng, least, top_value):
    extent = result.shape
    spot = [jax.random.randint(jax.random.fold_in(rng, axis), (), 0, extent[axis]) for axis in range(len(extent))]
    result = result.at[tuple(spot)].set(least)
    longest = extent.index(max(extent))
    spot[longest] = (spot[longest] + 1) % extent[longest]
    return result.at[tuple(spot)].set(top_value)


def levels(stream_key, shape, pieces, least, largest):
    level = 1.0
    for dim, shards_of in pieces:
        heights = jax.random.uniform(jax.random.fold_in(jax.random.fold_in(stream_key, 6), dim), (shards_of,), jnp.float32, least / len(pieces), largest / len(pieces))
        level = level * jnp.repeat(jnp.exp(heights), shape[dim] // shards_of).reshape((-1,) + (1,) * (len(shape) - 1 - dim))
    return level


def normal_values(own_key, extent, spread, limit, shards=(), held_as=jnp.bfloat16):
    level = levels(own_key, extent, shards, -0.22, 0.18) if shards else 1.0
    array = jax.random.normal(own_key, extent, jnp.float32) * spread * level
    return jnp.minimum(jnp.maximum(array, -limit), limit).astype(held_as)


def setup_inputs(seed: int = 0, part: int = 0) -> dict:
    keys = jax.random.split(jax.random.key(seed), 11)
    part_keys = jax.random.split(jax.random.fold_in(keys[10], part), 11)
    coef = jnp.clip(0.05 + 0.14 * jax.random.uniform(part_keys[0], (NX, NY, NZ), jnp.float32) ** levels(part_keys[0], (NX, NY, NZ), ((0, 8),), -0.2, 0.2), 0.05, 0.19)
    fwd_prev = normal_values(part_keys[1], (SUPERS, NX, NY, NZ), 0.2, 1.2, ((0, 2), (1, 8)), jnp.float32)
    fwd_now = normal_values(part_keys[2], (SUPERS, NX, NY, NZ), 0.2, 1.2, ((0, 2), (1, 8)), jnp.float32)
    adj_next = normal_values(part_keys[3], (SUPERS, NX, NY, NZ), 0.2, 1.2, ((0, 2), (1, 8)), jnp.float32)
    adj_after = normal_values(part_keys[4], (SUPERS, NX, NY, NZ), 0.2, 1.2, ((0, 2), (1, 8)), jnp.float32)
    encode = normal_values(part_keys[5], (SUPERS, SHOTS), 1.0, 4.0, ((0, 2),), jnp.float32)
    wavelet = normal_values(part_keys[6], (STEPS, SHOTS), 1.0, 4.0, (), jnp.float32)
    shot_cells = set_ends(jax.random.randint(part_keys[7], (SHOTS,), 0, NX * NY * NZ), jax.random.fold_in(part_keys[7], 1), 0, (NX * NY * NZ) - 1).astype(jnp.int32)
    rec_cells = set_ends(jax.random.randint(part_keys[8], (REC,), 0, NX * NY * NZ), jax.random.fold_in(part_keys[8], 1), 0, (NX * NY * NZ) - 1).astype(jnp.int32)
    records = normal_values(part_keys[9], (SUPERS, STEPS, REC), 0.2, 1.2, ((0, 2),), jnp.float32)
    return dict(coef=coef, fwd_prev=fwd_prev, fwd_now=fwd_now, adj_next=adj_next, adj_after=adj_after, encode=encode, wavelet=wavelet, shot_cells=shot_cells, rec_cells=rec_cells, records=records)


stencil_weights = (-205.0 / 72.0, 8.0 / 5.0, -1.0 / 5.0, 8.0 / 315.0, -1.0 / 560.0)


def laplace(extended):
    breadth = extended.shape[-3] - 8
    center = extended[..., 4:4 + breadth, :, :]
    across = center.shape[-2]
    downward = center.shape[-1]
    leading = [(0, 0)] * (center.ndim - 2)
    padded = jnp.pad(center, leading + [(4, 4), (4, 4)])
    summed = (3.0 * stencil_weights[0]) * center
    for offset in range(1, 5):
        along_x = extended[..., 4 + offset:4 + offset + breadth, :, :] + extended[..., 4 - offset:4 - offset + breadth, :, :]
        along_y = padded[..., 4 + offset:4 + offset + across, 4:4 + downward] + padded[..., 4 - offset:4 - offset + across, 4:4 + downward]
        along_z = padded[..., 4:4 + across, 4 + offset:4 + offset + downward] + padded[..., 4:4 + across, 4 - offset:4 - offset + downward]
        summed = summed + stencil_weights[offset] * (along_x + along_y + along_z)
    return summed


def pad_rows(field):
    return jnp.pad(field, [(0, 0), (4, 4), (0, 0), (0, 0)])


def reference(coef, fwd_prev, fwd_now, adj_next, adj_after, encode, wavelet, shot_cells, rec_cells, records):
    supers = fwd_now.shape[0]
    earlier, current = fwd_prev, fwd_now
    history = []
    misfits = []
    for index in range(STEPS):
        laplacian = laplace(pad_rows(current))
        updated = 2.0 * current - earlier + coef[None] * laplacian
        updated = updated.reshape(supers, -1).at[:, shot_cells].add(encode * wavelet[index][None, :]).reshape(current.shape)
        misfit = updated.reshape(supers, -1)[:, rec_cells] - records[:, index]
        history.append(laplacian)
        misfits.append(misfit)
        earlier, current = current, updated
    later, latest = adj_next, adj_after
    gradient = jnp.zeros(coef.shape, jnp.float32)
    for index in reversed(range(STEPS)):
        adjoint = 2.0 * later - latest + laplace(pad_rows(coef[None] * later))
        adjoint = adjoint.reshape(supers, -1).at[:, rec_cells].add(misfits[index]).reshape(later.shape)
        gradient = gradient + jnp.sum(adjoint * history[index], axis=0)
        latest, later = later, adjoint
    return gradient
```

```python
import functools

import jax
import jax.numpy as jnp
import numpy as np
from jax import lax
from jax.experimental import pallas as pl
from jax.experimental.pallas import tpu as pltpu
from jax.sharding import PartitionSpec as P

stencil_weights = (-205.0 / 72.0, 8.0 / 5.0, -1.0 / 5.0, 8.0 / 315.0, -1.0 / 560.0)
scaled_weights = (8064.0, -1008.0, 128.0, -9.0)
MESH = pl.DeviceIdType.MESH
f32 = jnp.float32
bf16 = jnp.bfloat16


def split(value):
    high = value.astype(bf16)
    low = (value - high.astype(f32)).astype(bf16)
    return high, low


def dot(a, b):
    return jnp.dot(a, b, preferred_element_type=f32)


def kernel(
    count,
    coef_in,
    prev_in,
    now_in,
    next_in,
    after_in,
    band,
    pick,
    place,
    shot_place,
    rec_depth,
    shot_amounts,
    observed,
    grad,
    field,
    adj,
    coef,
    history,
    sampled,
    misfit,
    in_local,
    in_send,
    in_recv,
    face_send,
    face_recv,
):
    steps = history.shape[0]
    layers, rows, depth = coef.shape
    half = layers // 2
    me = lax.axis_index("space")
    side = lax.rem(me, 2)
    partner = me + 1 - 2 * side
    has_left = me >= 2
    has_right = me < count - 2

    for slot in range(2):
        field[slot, 0:4] = jnp.zeros((4,) + field.shape[2:], f32)
        field[slot, layers + 4 : layers + 8] = jnp.zeros((4,) + field.shape[2:], f32)

        @pl.loop(0, layers)
        def _(x):
            field[slot, x + 4, 0:8] = jnp.zeros((8, depth), f32)
            field[slot, x + 4, rows + 8 : rows + 16] = jnp.zeros((8, depth), f32)

    barrier = pltpu.get_barrier_semaphore()
    pl.semaphore_signal(barrier, inc=1, device_id={"space": partner}, device_id_type=MESH)

    @pl.when(has_left)
    def _():
        pl.semaphore_signal(barrier, inc=1, device_id={"space": me - 2}, device_id_type=MESH)

    @pl.when(has_right)
    def _():
        pl.semaphore_signal(barrier, inc=1, device_id={"space": me + 2}, device_id_type=MESH)

    peers = 1 + jnp.where(has_left, 1, 0) + jnp.where(has_right, 1, 0)
    pl.semaphore_wait(barrier, peers)

    first = pl.multiple_of(side * half, half)
    keep = pl.multiple_of(side * rows, rows)
    give = pl.multiple_of(rows - side * rows, rows)
    targets = (
        (now_in, field.at[0, pl.ds(4 + first, half), pl.ds(8, rows)]),
        (prev_in, field.at[1, pl.ds(4 + first, half), pl.ds(8, rows)]),
        (coef_in, coef.at[pl.ds(first, half)]),
        (next_in, adj.at[0, pl.ds(first, half)]),
        (after_in, adj.at[1, pl.ds(first, half)]),
    )
    arriving = []
    for index, (source, target) in enumerate(targets):
        away = pltpu.make_async_remote_copy(
            src_ref=source.at[:, pl.ds(give, rows)],
            dst_ref=target,
            send_sem=in_send.at[index],
            recv_sem=in_recv.at[index],
            device_id={"space": partner},
            device_id_type=MESH,
        )
        here = pltpu.make_async_copy(
            source.at[:, pl.ds(keep, rows)], target, in_local.at[index]
        )
        away.start()
        here.start()
        arriving.append((away, here))

    def arrive(index):
        away, here = arriving[index]
        here.wait()
        away.wait()

    def faces(slot):
        near = pl.multiple_of((rows - 8) * (1 - side) + 8, 8)
        far = pl.multiple_of((rows + 8) * side, 8)
        inner = pl.ds(8, rows)
        to_left = pltpu.make_async_remote_copy(
            src_ref=field.at[slot, pl.ds(4, 4), inner],
            dst_ref=field.at[slot, pl.ds(layers + 4, 4), inner],
            send_sem=face_send.at[0, slot],
            recv_sem=face_recv.at[0, slot],
            device_id={"space": me - 2},
            device_id_type=MESH,
        )
        to_right = pltpu.make_async_remote_copy(
            src_ref=field.at[slot, pl.ds(layers, 4), inner],
            dst_ref=field.at[slot, pl.ds(0, 4), inner],
            send_sem=face_send.at[1, slot],
            recv_sem=face_recv.at[1, slot],
            device_id={"space": me + 2},
            device_id_type=MESH,
        )
        across = pltpu.make_async_remote_copy(
            src_ref=field.at[slot, pl.ds(4, layers), pl.ds(near, 8)],
            dst_ref=field.at[slot, pl.ds(4, layers), pl.ds(far, 8)],
            send_sem=face_send.at[2, slot],
            recv_sem=face_recv.at[2, slot],
            device_id={"space": partner},
            device_id_type=MESH,
        )
        return to_left, to_right, across

    def send_faces(slot):
        to_left, to_right, across = faces(slot)
        pl.when(has_left)(to_left.start)
        pl.when(has_right)(to_right.start)
        across.start()

    def receive_faces(slot):
        to_left, to_right, across = faces(slot)

        @pl.when(has_left)
        def _():
            to_left.wait_send()
            to_right.wait_recv()

        @pl.when(has_right)
        def _():
            to_right.wait_send()
            to_left.wait_recv()

        across.wait()

    block = 8
    lines = block * rows

    def flat(value):
        return value.reshape(lines, depth)

    def sample(slot, step):
        @pl.loop(0, layers // block)
        def _(c):
            part = field[slot, pl.ds(4 + c * block, block), 8 : rows + 8, :]
            high, low = split(flat(part))
            chooser = pick[c]
            found = dot(chooser, high) + dot(chooser, low)

            @pl.when(c == 0)
            def _():
                sampled[...] = found

            @pl.when(c > 0)
            def _():
                sampled[...] += found

        value = jnp.sum(sampled[...] * rec_depth[...], axis=1, keepdims=True)
        lane = lax.broadcasted_iota(jnp.int32, misfit.shape, 1)
        misfit[...] = jnp.where(lane == step, value, misfit[...])

    def depthwise(value):
        high, low = split(flat(value))
        along = dot(high, band[...]) + dot(low, band[...])
        return along.reshape(value.shape) * (1.0 / 5040.0) + (3.0 * stencil_weights[0]) * value

    def add_sides(slot, x, total):
        wide = field[slot, 4 + x]
        for offset in range(1, 5):
            beside = pltpu.roll(wide, offset, 0) + pltpu.roll(wide, rows + 16 - offset, 0)
            pair = field[slot, 4 + x + offset, 8 : rows + 8] + field[slot, 4 + x - offset, 8 : rows + 8]
            total = total + stencil_weights[offset] * (pair + beside[8 : rows + 8])
        return total

    arrive(0)
    arrive(1)
    arrive(2)
    misfit[...] = jnp.zeros_like(misfit)

    @pl.loop(0, steps)
    def _(step):
        slot = lax.rem(step, 2)
        other = 1 - slot
        send_faces(slot)

        @pl.when(step > 0)
        def _():
            sample(slot, step - 1)

        amount_high, amount_low = split(shot_amounts[step])

        @pl.loop(0, layers // block)
        def _(c):
            span = pl.ds(c * block, block)
            mid = pl.ds(4 + c * block, block)
            value = field[slot, mid, 8 : rows + 8, :]
            history[step, span] = depthwise(value)
            spots = shot_place[c]
            shots = dot(spots, amount_high) + dot(spots, amount_low)
            before = field[other, mid, 8 : rows + 8, :]
            field[other, mid, 8 : rows + 8, :] = 2.0 * value - before + shots.reshape(value.shape)

        receive_faces(slot)

        @pl.loop(0, layers)
        def _(x):
            total = add_sides(slot, x, history[step, x])
            history[step, x] = total
            field[other, 4 + x, 8 : rows + 8] += coef[x] * total

    last = steps % 2
    sample(last, steps - 1)
    misfit[...] = misfit[...] - observed[...]
    arrive(3)
    arrive(4)

    @pl.loop(0, layers)
    def _(x):
        field[last, 4 + x, 8 : rows + 8] = coef[x] * adj[0, x]
        grad[x] = jnp.zeros((rows, depth), f32)

    @pl.loop(0, steps)
    def _(back):
        slot = lax.rem(back + steps, 2)
        other = 1 - slot
        later = lax.rem(back, 2)
        latest = 1 - later
        step = steps - 1 - back
        send_faces(slot)
        lane = lax.broadcasted_iota(jnp.int32, misfit.shape, 1)
        amount = jnp.sum(jnp.where(lane == step, misfit[...], 0.0), axis=1, keepdims=True)
        amount_high, amount_low = split(amount * rec_depth[...])

        @pl.loop(0, layers // block)
        def _(c):
            span = pl.ds(c * block, block)
            value = field[slot, pl.ds(4 + c * block, block), 8 : rows + 8, :]
            spots = place[c]
            added = dot(spots, amount_high) + dot(spots, amount_low)
            adj[latest, span] = (
                2.0 * adj[later, span] - adj[latest, span] + depthwise(value) + added.reshape(value.shape)
            )

        receive_faces(slot)

        @pl.loop(0, layers)
        def _(x):
            total = add_sides(slot, x, adj[latest, x])
            adj[latest, x] = total
            field[other, 4 + x, 8 : rows + 8] = coef[x] * total
            grad[x] += total * history[step, x]


def shards(
    count, coef, fwd_prev, fwd_now, adj_next, adj_after, encode, wavelet, shot_cells, rec_cells, records
):
    thick, across, depth = coef.shape
    steps, shots = wavelet.shape
    receivers = rec_cells.shape[0]
    layers, rows = 2 * thick, across // 2
    me = lax.axis_index("space")
    block = 8
    chunks, lines = layers // block, block * rows

    def locate(cells):
        x = cells // (across * depth) - (me // 2) * layers
        y = (cells // depth) % across - (me % 2) * rows
        inside = (x >= 0) & (x < layers) & (y >= 0) & (y < rows)
        return jnp.where(inside, x * rows + y, -1), cells % depth

    rec_line, rec_z = locate(rec_cells)
    shot_line, shot_z = locate(shot_cells)
    width = -(-shots // 128) * 128
    shot_line = jnp.pad(shot_line, (0, width - shots), constant_values=-1)
    every = jnp.arange(layers * rows, dtype=jnp.int32).reshape(chunks, lines)
    pick = (rec_line[None, :, None] == every[:, None, :]).astype(bf16)
    place = (every[:, :, None] == rec_line[None, None, :]).astype(bf16)
    shot_place = (every[:, :, None] == shot_line[None, None, :]).astype(bf16)
    level = jnp.arange(depth, dtype=jnp.int32)
    rec_depth = (rec_z[:, None] == level[None, :]).astype(f32)
    amounts = encode[0][None, :] * wavelet
    shot_amounts = jnp.where(shot_z[None, :, None] == level[None, None, :], amounts[:, :, None], 0.0)
    shot_amounts = jnp.pad(shot_amounts, ((0, 0), (0, width - shots), (0, 0)))
    observed = jnp.pad(records[0].T, ((0, 0), (0, 128 - steps)))
    band = np.zeros((depth, depth), np.float32)
    for offset in range(1, 5):
        band += scaled_weights[offset - 1] * (np.eye(depth, k=offset) + np.eye(depth, k=-offset))

    vmem = pl.BlockSpec(memory_space=pltpu.VMEM)
    hbm = pl.BlockSpec(memory_space=pl.ANY)
    partial = pl.pallas_call(
        functools.partial(kernel, count),
        out_shape=jax.ShapeDtypeStruct((layers, rows, depth), f32),
        in_specs=[hbm] * 5 + [vmem] * 7,
        out_specs=vmem,
        scratch_shapes=[
            pltpu.VMEM((2, layers + 8, rows + 16, depth), f32),
            pltpu.VMEM((2, layers, rows, depth), f32),
            pltpu.VMEM((layers, rows, depth), f32),
            pltpu.VMEM((steps, layers, rows, depth), f32),
            pltpu.VMEM((receivers, depth), f32),
            pltpu.VMEM((receivers, 128), f32),
            pltpu.SemaphoreType.DMA((5,)),
            pltpu.SemaphoreType.DMA((5,)),
            pltpu.SemaphoreType.DMA((5,)),
            pltpu.SemaphoreType.DMA((3, 2)),
            pltpu.SemaphoreType.DMA((3, 2)),
        ],
        compiler_params=pltpu.CompilerParams(
            collective_id=0, has_side_effects=True, vmem_limit_bytes=60 * 1024 * 1024
        ),
    )(
        coef,
        fwd_prev[0],
        fwd_now[0],
        adj_next[0],
        adj_after[0],
        jnp.asarray(band, bf16),
        pick,
        place,
        shot_place,
        rec_depth,
        shot_amounts,
        observed,
    )
    summed = lax.psum_scatter(partial, "shot", scatter_dimension=0, tiled=True)
    moves = [
        (s * count + 2 * q + b, b * count + 2 * q + s)
        for q in range(count // 2)
        for b in range(2)
        for s in range(2)
    ]
    return lax.ppermute(summed, ("shot", "space"), moves)


def solution(mesh):
    placed = (
        P(("groups", "space"), None, None),
        P(("groups", "shot"), "space", None, None),
        P(("groups", "shot"), "space", None, None),
        P(("groups", "shot"), "space", None, None),
        P(("groups", "shot"), "space", None, None),
        P(("groups", "shot"), None),
        P("groups", None),
        P("groups"),
        P("groups"),
        P(("groups", "shot"), None, None),
    )
    return jax.shard_map(
        functools.partial(shards, mesh.shape["space"]),
        mesh=mesh,
        in_specs=placed,
        out_specs=P(("groups", "space"), "shot", None),
        check_vma=False,
    )
```

```python
import functools

import jax
import jax.numpy as jnp
import numpy as np
from jax import lax
from jax.experimental import pallas as pl
from jax.experimental.pallas import tpu as pltpu
from jax.sharding import PartitionSpec as P

stencil_weights = (-205.0 / 72.0, 8.0 / 5.0, -1.0 / 5.0, 8.0 / 315.0, -1.0 / 560.0)
scaled_weights = (8064.0, -1008.0, 128.0, -9.0)
MESH = pl.DeviceIdType.MESH
f32 = jnp.float32
bf16 = jnp.bfloat16


def split(value):
    high = value.astype(bf16)
    low = (value - high.astype(f32)).astype(bf16)
    return high, low


def dot(a, b):
    return jnp.dot(a, b, preferred_element_type=f32)


def kernel(
    count,
    coef_in,
    prev_in,
    now_in,
    next_in,
    after_in,
    band,
    pick,
    place,
    shot_place,
    rec_depth,
    shot_amounts,
    observed,
    grad,
    field,
    adj,
    coef,
    history,
    sampled,
    misfit,
    in_local,
    in_send,
    in_recv,
    twin_send,
    twin_recv,
    face_send,
    face_recv,
):
    steps = history.shape[0]
    layers, rows, depth = coef.shape
    half = layers // 2
    me = lax.axis_index("space")
    core = lax.axis_index("shot")
    side = lax.rem(me, 2)
    partner = me + 1 - 2 * side
    has_left = me >= 2
    has_right = me < count - 2

    for slot in range(2):
        field[slot, 0:4] = jnp.zeros((4,) + field.shape[2:], f32)
        field[slot, layers + 4 : layers + 8] = jnp.zeros((4,) + field.shape[2:], f32)

        @pl.loop(0, layers)
        def _(x):
            field[slot, x + 4, 0:8] = jnp.zeros((8, depth), f32)
            field[slot, x + 4, rows + 8 : rows + 16] = jnp.zeros((8, depth), f32)

    barrier = pltpu.get_barrier_semaphore()
    pl.semaphore_signal(barrier, inc=1, device_id={"space": partner}, device_id_type=MESH)

    pl.semaphore_signal(barrier, inc=1, device_id={"shot": 1 - core}, device_id_type=MESH)

    @pl.when(has_left)
    def _():
        pl.semaphore_signal(barrier, inc=1, device_id={"space": me - 2}, device_id_type=MESH)

    @pl.when(has_right)
    def _():
        pl.semaphore_signal(barrier, inc=1, device_id={"space": me + 2}, device_id_type=MESH)

    peers = 2 + jnp.where(has_left, 1, 0) + jnp.where(has_right, 1, 0)
    pl.semaphore_wait(barrier, peers)

    first = pl.multiple_of(side * half, half)
    keep = pl.multiple_of(side * rows, rows)
    give = pl.multiple_of(rows - side * rows, rows)
    part = half // 2
    mine = pl.multiple_of(core * part, part)
    chunk = half // 8
    targets = (
        (now_in, field.at[0, pl.ds(4 + first, half), pl.ds(8, rows)]),
        (prev_in, field.at[1, pl.ds(4 + first, half), pl.ds(8, rows)]),
        (coef_in, coef.at[pl.ds(first, half)]),
        (next_in, adj.at[0, pl.ds(first, half)]),
        (after_in, adj.at[1, pl.ds(first, half)]),
    )

    def swap(index, start, size):
        source, target = targets[index]
        return pltpu.make_async_remote_copy(
            src_ref=source.at[pl.ds(start, size), pl.ds(give, rows)],
            dst_ref=target.at[pl.ds(start, size)],
            send_sem=in_send.at[index],
            recv_sem=in_recv.at[index],
            device_id={"space": partner},
            device_id_type=MESH,
        )

    def stay(index):
        source, target = targets[index]
        return pltpu.make_async_copy(source.at[:, pl.ds(keep, rows)], target, in_local.at[index])

    def arrive(index):
        stay(index).wait()
        swap(index, 0, half).wait()

    swap(0, 0, half).start()
    swap(1, 0, half).start()
    swap(2, mine, part).start()
    for index in range(5):
        stay(index).start()

    def share():
        swap(2, mine, part).wait()
        received = coef.at[pl.ds(half - first + mine, part)]
        return pltpu.make_async_remote_copy(
            src_ref=received,
            dst_ref=received,
            send_sem=twin_send,
            recv_sem=twin_recv,
            device_id={"shot": 1 - core},
            device_id_type=MESH,
        )

    def faces(slot):
        near = (rows - 4) * (1 - side) + 8
        far = rows * side + 8 * side + 4 * (1 - side)
        inner = pl.ds(8, rows)
        to_left = pltpu.make_async_remote_copy(
            src_ref=field.at[slot, pl.ds(4, 4), inner],
            dst_ref=field.at[slot, pl.ds(layers + 4, 4), inner],
            send_sem=face_send.at[0, slot],
            recv_sem=face_recv.at[0, slot],
            device_id={"space": me - 2},
            device_id_type=MESH,
        )
        to_right = pltpu.make_async_remote_copy(
            src_ref=field.at[slot, pl.ds(layers, 4), inner],
            dst_ref=field.at[slot, pl.ds(0, 4), inner],
            send_sem=face_send.at[1, slot],
            recv_sem=face_recv.at[1, slot],
            device_id={"space": me + 2},
            device_id_type=MESH,
        )
        across = pltpu.make_async_remote_copy(
            src_ref=field.at[slot, pl.ds(4, layers), pl.ds(near, 4)],
            dst_ref=field.at[slot, pl.ds(4, layers), pl.ds(far, 4)],
            send_sem=face_send.at[2, slot],
            recv_sem=face_recv.at[2, slot],
            device_id={"space": partner},
            device_id_type=MESH,
        )
        return to_left, to_right, across

    def send_faces(slot):
        to_left, to_right, across = faces(slot)
        pl.when(has_left)(to_left.start)
        pl.when(has_right)(to_right.start)
        across.start()

    def receive_faces(slot):
        to_left, to_right, across = faces(slot)

        @pl.when(has_left)
        def _():
            to_left.wait_send()
            to_right.wait_recv()

        @pl.when(has_right)
        def _():
            to_right.wait_send()
            to_left.wait_recv()

        across.wait()

    block = 8
    lines = block * rows

    def flat(value):
        return value.reshape(lines, depth)

    def store_sample(step):
        value = jnp.sum(sampled[...] * rec_depth[...], axis=1, keepdims=True)
        lane = lax.broadcasted_iota(jnp.int32, misfit.shape, 1)
        misfit[...] = jnp.where(lane == step, value, misfit[...])

    def add_sample(c, high, low):
        chooser = pick[c]
        found = dot(chooser, high) + dot(chooser, low)

        @pl.when(c == 0)
        def _():
            sampled[...] = found

        @pl.when(c > 0)
        def _():
            sampled[...] += found

    def depthwise(value, high, low):
        along = dot(high, band[...]) + dot(low, band[...])
        return along.reshape(value.shape) * (1.0 / 5040.0) + (3.0 * stencil_weights[0]) * value

    def add_sides(slot, x, low, tall, total):
        wide = field[slot, 4 + x, pl.ds(low, tall + 16)]
        here = pl.ds(pl.multiple_of(low + 8, 8), tall)
        for offset in range(1, 5):
            beside = pltpu.roll(wide, offset, 0) + pltpu.roll(wide, tall + 16 - offset, 0)
            pair = field[slot, 4 + x + offset, here] + field[slot, 4 + x - offset, here]
            total = total + stencil_weights[offset] * (pair + beside[8 : tall + 8])
        return total

    inner_low = pl.multiple_of(8 * side, 8)
    edge_low = pl.multiple_of((rows - 8) * (1 - side), 8)

    def rim(unit):
        @pl.loop(0, 4)
        def _(x):
            unit(x, 0, rows)
            unit(layers - 4 + x, 0, rows)

        @pl.loop(1, layers // 4 - 1)
        def _(x):
            for inside in range(4):
                unit(4 * x + inside, edge_low, 8)

    def interior(unit):
        @pl.loop(4, layers - 4)
        def _(x):
            unit(x, inner_low, rows - 8)

    misfit[...] = jnp.zeros_like(misfit)
    arrive(0)
    send_faces(0)
    arrive(1)

    @pl.loop(0, steps)
    def _(step):
        slot = lax.rem(step, 2)
        other = 1 - slot
        amount_high, amount_low = split(shot_amounts[step])

        @pl.when(step < 8)
        def _():
            swap(3, step * chunk, chunk).start()
            swap(4, step * chunk, chunk).start()

        @pl.loop(0, layers // block)
        def _(c):
            span = pl.ds(c * block, block)
            mid = pl.ds(4 + c * block, block)
            value = field[slot, mid, 8 : rows + 8, :]
            high, low = split(flat(value))
            history[step, span] = depthwise(value, high, low)
            spots = shot_place[c]
            shots = dot(spots, amount_high) + dot(spots, amount_low)
            before = field[other, mid, 8 : rows + 8, :]
            field[other, mid, 8 : rows + 8, :] = 2.0 * value - before + shots.reshape(value.shape)
            add_sample(c, high, low)

        store_sample(step - 1)

        @pl.when(step == 0)
        def _():
            stay(2).wait()
            passed = share()
            passed.start()
            passed.wait()

        receive_faces(slot)

        def unit(x, low, tall):
            mine = pl.ds(low, tall)
            total = add_sides(slot, x, low, tall, history[step, x, mine])
            history[step, x, mine] = total
            field[other, 4 + x, pl.ds(pl.multiple_of(low + 8, 8), tall)] += coef[x, mine] * total

        rim(unit)

        @pl.when(step < steps - 1)
        def _():
            send_faces(other)

        interior(unit)

    last = steps % 2

    @pl.loop(0, layers // block)
    def _(c):
        add_sample(c, *split(flat(field[last, pl.ds(4 + c * block, block), 8 : rows + 8, :])))

    store_sample(steps - 1)
    misfit[...] = misfit[...] - observed[...]
    arrive(3)
    arrive(4)

    @pl.loop(0, layers)
    def _(x):
        field[last, 4 + x, 8 : rows + 8] = coef[x] * adj[0, x]
        grad[x] = jnp.zeros((rows, depth), f32)

    send_faces(last)

    @pl.loop(0, steps)
    def _(back):
        slot = lax.rem(back + steps, 2)
        other = 1 - slot
        later = lax.rem(back, 2)
        latest = 1 - later
        step = steps - 1 - back
        lane = lax.broadcasted_iota(jnp.int32, misfit.shape, 1)
        amount = jnp.sum(jnp.where(lane == step, misfit[...], 0.0), axis=1, keepdims=True)
        amount_high, amount_low = split(amount * rec_depth[...])

        @pl.loop(0, layers // block)
        def _(c):
            span = pl.ds(c * block, block)
            value = field[slot, pl.ds(4 + c * block, block), 8 : rows + 8, :]
            spots = place[c]
            added = dot(spots, amount_high) + dot(spots, amount_low)
            adj[latest, span] = (
                2.0 * adj[later, span]
                - adj[latest, span]
                + depthwise(value, *split(flat(value)))
                + added.reshape(value.shape)
            )

        receive_faces(slot)

        def unit(x, low, tall):
            mine = pl.ds(low, tall)
            total = add_sides(slot, x, low, tall, adj[latest, x, mine])
            adj[latest, x, mine] = total
            field[other, 4 + x, pl.ds(pl.multiple_of(low + 8, 8), tall)] = coef[x, mine] * total
            grad[x, mine] += total * history[step, x, mine]

        rim(unit)

        @pl.when(back < steps - 1)
        def _():
            send_faces(other)

        interior(unit)


def shards(
    count, coef, fwd_prev, fwd_now, adj_next, adj_after, encode, wavelet, shot_cells, rec_cells, records
):
    thick, across, depth = coef.shape
    steps, shots = wavelet.shape
    receivers = rec_cells.shape[0]
    layers, rows = 2 * thick, across // 2
    me = lax.axis_index("space")
    block = 8
    chunks, lines = layers // block, block * rows

    def locate(cells):
        x = cells // (across * depth) - (me // 2) * layers
        y = (cells // depth) % across - (me % 2) * rows
        inside = (x >= 0) & (x < layers) & (y >= 0) & (y < rows)
        return jnp.where(inside, x * rows + y, -1), cells % depth

    rec_line, rec_z = locate(rec_cells)
    shot_line, shot_z = locate(shot_cells)
    width = -(-shots // 128) * 128
    shot_line = jnp.pad(shot_line, (0, width - shots), constant_values=-1)
    every = jnp.arange(layers * rows, dtype=jnp.int32).reshape(chunks, lines)
    pick = (rec_line[None, :, None] == every[:, None, :]).astype(bf16)
    place = (every[:, :, None] == rec_line[None, None, :]).astype(bf16)
    shot_place = (every[:, :, None] == shot_line[None, None, :]).astype(bf16)
    level = jnp.arange(depth, dtype=jnp.int32)
    rec_depth = (rec_z[:, None] == level[None, :]).astype(f32)
    amounts = encode[0][None, :] * wavelet
    shot_amounts = jnp.where(shot_z[None, :, None] == level[None, None, :], amounts[:, :, None], 0.0)
    shot_amounts = jnp.pad(shot_amounts, ((0, 0), (0, width - shots), (0, 0)))
    observed = jnp.pad(records[0].T, ((0, 0), (0, 128 - steps)))
    band = np.zeros((depth, depth), np.float32)
    for offset in range(1, 5):
        band += scaled_weights[offset - 1] * (np.eye(depth, k=offset) + np.eye(depth, k=-offset))

    vmem = pl.BlockSpec(memory_space=pltpu.VMEM)
    hbm = pl.BlockSpec(memory_space=pl.ANY)
    partial = pl.pallas_call(
        functools.partial(kernel, count),
        out_shape=jax.ShapeDtypeStruct((layers, rows, depth), f32),
        in_specs=[hbm] * 5 + [vmem] * 7,
        out_specs=vmem,
        scratch_shapes=[
            pltpu.VMEM((2, layers + 8, rows + 16, depth), f32),
            pltpu.VMEM((2, layers, rows, depth), f32),
            pltpu.VMEM((layers, rows, depth), f32),
            pltpu.VMEM((steps, layers, rows, depth), f32),
            pltpu.VMEM((receivers, depth), f32),
            pltpu.VMEM((receivers, 128), f32),
            pltpu.SemaphoreType.DMA((5,)),
            pltpu.SemaphoreType.DMA((5,)),
            pltpu.SemaphoreType.DMA((5,)),
            pltpu.SemaphoreType.DMA,
            pltpu.SemaphoreType.DMA,
            pltpu.SemaphoreType.DMA((3, 2)),
            pltpu.SemaphoreType.DMA((3, 2)),
        ],
        compiler_params=pltpu.CompilerParams(
            collective_id=0, has_side_effects=True, vmem_limit_bytes=60 * 1024 * 1024
        ),
    )(
        coef,
        fwd_prev[0],
        fwd_now[0],
        adj_next[0],
        adj_after[0],
        jnp.asarray(band, bf16),
        pick,
        place,
        shot_place,
        rec_depth,
        shot_amounts,
        observed,
    )
    summed = lax.psum_scatter(partial, "shot", scatter_dimension=0, tiled=True)
    moves = [
        (s * count + 2 * q + b, b * count + 2 * q + s)
        for q in range(count // 2)
        for b in range(2)
        for s in range(2)
    ]
    return lax.ppermute(summed, ("shot", "space"), moves)


def solution(mesh):
    placed = (
        P(("groups", "space"), None, None),
        P(("groups", "shot"), "space", None, None),
        P(("groups", "shot"), "space", None, None),
        P(("groups", "shot"), "space", None, None),
        P(("groups", "shot"), "space", None, None),
        P(("groups", "shot"), None),
        P("groups", None),
        P("groups"),
        P("groups"),
        P(("groups", "shot"), None, None),
    )
    return jax.shard_map(
        functools.partial(shards, mesh.shape["space"]),
        mesh=mesh,
        in_specs=placed,
        out_specs=P(("groups", "space"), "shot", None),
        check_vma=False,
    )
```

```python
import functools

import jax
import jax.numpy as jnp
import numpy as np
from jax import lax
from jax.experimental import pallas as pl
from jax.experimental.pallas import tpu as pltpu
from jax.sharding import PartitionSpec as P

stencil_weights = (-205.0 / 72.0, 8.0 / 5.0, -1.0 / 5.0, 8.0 / 315.0, -1.0 / 560.0)
scaled_weights = (8064.0, -1008.0, 128.0, -9.0)
MESH = pl.DeviceIdType.MESH
f32 = jnp.float32
bf16 = jnp.bfloat16


def split(value):
    high = value.astype(bf16)
    low = (value - high.astype(f32)).astype(bf16)
    return high, low


def dot(a, b):
    return jnp.dot(a, b, preferred_element_type=f32)


def kernel(
    count,
    coef_in,
    prev_in,
    now_in,
    next_in,
    after_in,
    band,
    rec_line,
    rec_column,
    rec_level,
    shot_line,
    shot_level,
    shot_amounts,
    observed,
    out,
    pick,
    place,
    shot_place,
    rec_depth,
    grad,
    twin_grad,
    field,
    adj,
    coef,
    history,
    sampled,
    misfit,
    in_local,
    in_send,
    in_recv,
    twin_send,
    twin_recv,
    face_send,
    face_recv,
    half_send,
    half_recv,
    out_send,
    out_recv,
):
    steps = history.shape[0]
    layers, rows, depth = coef.shape
    half = layers // 2
    me = lax.axis_index("space")
    core = lax.axis_index("shot")
    side = lax.rem(me, 2)
    partner = me + 1 - 2 * side
    has_left = me >= 2
    has_right = me < count - 2

    for slot in range(2):
        field[slot, 0:4] = jnp.zeros((4,) + field.shape[2:], f32)
        field[slot, layers + 4 : layers + 8] = jnp.zeros((4,) + field.shape[2:], f32)

        @pl.loop(0, layers)
        def _(x):
            field[slot, x + 4, 0:8] = jnp.zeros((8, depth), f32)
            field[slot, x + 4, rows + 8 : rows + 16] = jnp.zeros((8, depth), f32)

    barrier = pltpu.get_barrier_semaphore()
    pl.semaphore_signal(barrier, inc=1, device_id={"space": partner}, device_id_type=MESH)

    pl.semaphore_signal(barrier, inc=1, device_id={"shot": 1 - core}, device_id_type=MESH)

    @pl.when(has_left)
    def _():
        pl.semaphore_signal(barrier, inc=1, device_id={"space": me - 2}, device_id_type=MESH)

    @pl.when(has_right)
    def _():
        pl.semaphore_signal(barrier, inc=1, device_id={"space": me + 2}, device_id_type=MESH)

    crossed = side != core
    owner = {"space": partner, "shot": 1 - core}

    @pl.when(crossed)
    def _():
        pl.semaphore_signal(barrier, inc=1, device_id=owner, device_id_type=MESH)

    peers = 2 + jnp.where(crossed, 1, 0) + jnp.where(has_left, 1, 0) + jnp.where(has_right, 1, 0)
    pl.semaphore_wait(barrier, peers)

    first = pl.multiple_of(side * half, half)
    keep = pl.multiple_of(side * rows, rows)
    give = pl.multiple_of(rows - side * rows, rows)
    part = half // 2
    mine = pl.multiple_of(core * part, part)
    chunk = half // 8
    targets = (
        (now_in, field.at[0, pl.ds(4 + first, half), pl.ds(8, rows)]),
        (prev_in, field.at[1, pl.ds(4 + first, half), pl.ds(8, rows)]),
        (coef_in, coef.at[pl.ds(first, half)]),
        (next_in, adj.at[0, pl.ds(first, half)]),
        (after_in, adj.at[1, pl.ds(first, half)]),
    )

    def swap(index, start, size):
        source, target = targets[index]
        return pltpu.make_async_remote_copy(
            src_ref=source.at[pl.ds(start, size), pl.ds(give, rows)],
            dst_ref=target.at[pl.ds(start, size)],
            send_sem=in_send.at[index],
            recv_sem=in_recv.at[index],
            device_id={"space": partner},
            device_id_type=MESH,
        )

    def stay(index):
        source, target = targets[index]
        return pltpu.make_async_copy(source.at[:, pl.ds(keep, rows)], target, in_local.at[index])

    def arrive(index):
        stay(index).wait()
        swap(index, 0, half).wait()

    swap(0, 0, half).start()
    swap(1, 0, half).start()
    swap(2, mine, part).start()
    for index in range(5):
        stay(index).start()

    def share():
        swap(2, mine, part).wait()
        received = coef.at[pl.ds(half - first + mine, part)]
        return pltpu.make_async_remote_copy(
            src_ref=received,
            dst_ref=received,
            send_sem=twin_send,
            recv_sem=twin_recv,
            device_id={"shot": 1 - core},
            device_id_type=MESH,
        )

    def faces(slot):
        near = (rows - 4) * (1 - side) + 8
        far = rows * side + 8 * side + 4 * (1 - side)
        inner = pl.ds(8, rows)
        to_left = pltpu.make_async_remote_copy(
            src_ref=field.at[slot, pl.ds(4, 4), inner],
            dst_ref=field.at[slot, pl.ds(layers + 4, 4), inner],
            send_sem=face_send.at[0, slot],
            recv_sem=face_recv.at[0, slot],
            device_id={"space": me - 2},
            device_id_type=MESH,
        )
        to_right = pltpu.make_async_remote_copy(
            src_ref=field.at[slot, pl.ds(layers, 4), inner],
            dst_ref=field.at[slot, pl.ds(0, 4), inner],
            send_sem=face_send.at[1, slot],
            recv_sem=face_recv.at[1, slot],
            device_id={"space": me + 2},
            device_id_type=MESH,
        )
        across = pltpu.make_async_remote_copy(
            src_ref=field.at[slot, pl.ds(4, layers), pl.ds(near, 4)],
            dst_ref=field.at[slot, pl.ds(4, layers), pl.ds(far, 4)],
            send_sem=face_send.at[2, slot],
            recv_sem=face_recv.at[2, slot],
            device_id={"space": partner},
            device_id_type=MESH,
        )
        return to_left, to_right, across

    def send_faces(slot):
        to_left, to_right, across = faces(slot)
        pl.when(has_left)(to_left.start)
        pl.when(has_right)(to_right.start)
        across.start()

    def receive_faces(slot):
        to_left, to_right, across = faces(slot)

        @pl.when(has_left)
        def _():
            to_left.wait_send()
            to_right.wait_recv()

        @pl.when(has_right)
        def _():
            to_right.wait_send()
            to_left.wait_recv()

        across.wait()

    block = 8
    lines = block * rows

    def flat(value):
        return value.reshape(lines, depth)

    def store_sample(step):
        value = jnp.sum(sampled[...] * rec_depth[...], axis=1, keepdims=True)
        lane = lax.broadcasted_iota(jnp.int32, misfit.shape, 1)
        misfit[...] = jnp.where(lane == step, value, misfit[...])

    def add_sample(c, high, low):
        chooser = pick[c]
        found = dot(chooser, high) + dot(chooser, low)

        @pl.when(c == 0)
        def _():
            sampled[...] = found

        @pl.when(c > 0)
        def _():
            sampled[...] += found

    def depthwise(value, high, low):
        along = dot(high, band[...]) + dot(low, band[...])
        return along.reshape(value.shape) * (1.0 / 5040.0) + (3.0 * stencil_weights[0]) * value

    def add_sides(slot, x, low, tall, total):
        wide = field[slot, 4 + x, pl.ds(low, tall + 16)]
        here = pl.ds(pl.multiple_of(low + 8, 8), tall)
        for offset in range(1, 5):
            beside = pltpu.roll(wide, offset, 0) + pltpu.roll(wide, tall + 16 - offset, 0)
            pair = field[slot, 4 + x + offset, here] + field[slot, 4 + x - offset, here]
            total = total + stencil_weights[offset] * (pair + beside[8 : tall + 8])
        return total

    inner_low = pl.multiple_of(8 * side, 8)
    edge_low = pl.multiple_of((rows - 8) * (1 - side), 8)

    def rim(unit):
        @pl.loop(0, 4)
        def _(x):
            unit(x, 0, rows)
            unit(layers - 4 + x, 0, rows)

        @pl.loop(1, layers // 4 - 1)
        def _(x):
            for inside in range(4):
                unit(4 * x + inside, edge_low, 8)

    def interior(unit):
        @pl.loop(4, layers - 4)
        def _(x):
            unit(x, inner_low, rows - 8)

    misfit[...] = jnp.zeros_like(misfit)

    def one_hot(index, shape, axis, start, kind):
        hit = lax.broadcasted_iota(jnp.int32, shape, axis) + start == index
        return jnp.where(hit, 1.0, 0.0).astype(kind)

    receivers, shots_held = rec_depth.shape[0], shot_place.shape[2]
    rec_depth[...] = one_hot(rec_level[...], rec_depth.shape, 1, 0, f32)

    @pl.loop(0, layers // block)
    def _(c):
        start = c * lines
        pick[c] = one_hot(rec_column[...], (receivers, lines), 1, start, bf16)
        place[c] = one_hot(rec_line[...], (lines, receivers), 0, start, bf16)
        shot_place[c] = one_hot(shot_line[...], (lines, shots_held), 0, start, bf16)

    arrive(0)
    send_faces(0)
    arrive(1)

    @pl.loop(0, steps)
    def _(step):
        slot = lax.rem(step, 2)
        other = 1 - slot
        shot_lane = lax.broadcasted_iota(jnp.int32, shot_amounts.shape, 1)
        shot_amount = jnp.sum(jnp.where(shot_lane == step, shot_amounts[...], 0.0), axis=1, keepdims=True)
        shot_depth = one_hot(shot_level[...], (shots_held, depth), 1, 0, f32)
        amount_high, amount_low = split(shot_amount * shot_depth)

        @pl.when(step < 8)
        def _():
            swap(3, step * chunk, chunk).start()
            swap(4, step * chunk, chunk).start()

        @pl.loop(0, layers // block)
        def _(c):
            span = pl.ds(c * block, block)
            mid = pl.ds(4 + c * block, block)
            value = field[slot, mid, 8 : rows + 8, :]
            high, low = split(flat(value))
            history[step, span] = depthwise(value, high, low)
            spots = shot_place[c]
            shots = dot(spots, amount_high) + dot(spots, amount_low)
            before = field[other, mid, 8 : rows + 8, :]
            field[other, mid, 8 : rows + 8, :] = 2.0 * value - before + shots.reshape(value.shape)
            add_sample(c, high, low)

        store_sample(step - 1)

        @pl.when(step == 0)
        def _():
            stay(2).wait()
            passed = share()
            passed.start()
            passed.wait()

        receive_faces(slot)

        def unit(x, low, tall):
            mine = pl.ds(low, tall)
            total = add_sides(slot, x, low, tall, history[step, x, mine])
            history[step, x, mine] = total
            field[other, 4 + x, pl.ds(pl.multiple_of(low + 8, 8), tall)] += coef[x, mine] * total

        rim(unit)

        @pl.when(step < steps - 1)
        def _():
            send_faces(other)

        interior(unit)

    last = steps % 2

    @pl.loop(0, layers // block)
    def _(c):
        add_sample(c, *split(flat(field[last, pl.ds(4 + c * block, block), 8 : rows + 8, :])))

    store_sample(steps - 1)
    misfit[...] = misfit[...] - observed[...]
    arrive(3)
    arrive(4)

    @pl.loop(0, layers)
    def _(x):
        field[last, 4 + x, 8 : rows + 8] = coef[x] * adj[0, x]
        grad[x] = jnp.zeros((rows, depth), f32)

    send_faces(last)

    @pl.loop(0, steps)
    def _(back):
        slot = lax.rem(back + steps, 2)
        other = 1 - slot
        later = lax.rem(back, 2)
        latest = 1 - later
        step = steps - 1 - back
        lane = lax.broadcasted_iota(jnp.int32, misfit.shape, 1)
        amount = jnp.sum(jnp.where(lane == step, misfit[...], 0.0), axis=1, keepdims=True)
        amount_high, amount_low = split(amount * rec_depth[...])

        @pl.loop(0, layers // block)
        def _(c):
            span = pl.ds(c * block, block)
            value = field[slot, pl.ds(4 + c * block, block), 8 : rows + 8, :]
            spots = place[c]
            added = dot(spots, amount_high) + dot(spots, amount_low)
            adj[latest, span] = (
                2.0 * adj[later, span]
                - adj[latest, span]
                + depthwise(value, *split(flat(value)))
                + added.reshape(value.shape)
            )

        receive_faces(slot)

        def unit(x, low, tall):
            mine = pl.ds(low, tall)
            total = add_sides(slot, x, low, tall, adj[latest, x, mine])
            adj[latest, x, mine] = total
            field[other, 4 + x, pl.ds(pl.multiple_of(low + 8, 8), tall)] = coef[x, mine] * total
            grad[x, mine] += total * history[step, x, mine]

        @pl.when(back < steps - 1)
        def _():
            rim(unit)
            send_faces(other)
            interior(unit)

        @pl.when(back == steps - 1)
        def _():
            own = pl.multiple_of(core * half, half)
            handed = half - own

            @pl.loop(0, half)
            def _(x):
                unit(handed + x, 0, rows)

            halves = pltpu.make_async_remote_copy(
                src_ref=grad.at[pl.ds(handed, half)],
                dst_ref=twin_grad,
                send_sem=half_send,
                recv_sem=half_recv,
                device_id={"shot": 1 - core},
                device_id_type=MESH,
            )
            halves.start()

            @pl.loop(0, half)
            def _(x):
                unit(own + x, 0, rows)

            halves.wait()

            @pl.when(jnp.logical_not(crossed))
            def _():
                @pl.loop(0, half)
                def _(x):
                    out[x] = grad[own + x] + twin_grad[x]

            @pl.when(crossed)
            def _():
                size = half // 4

                @pl.loop(0, 4)
                def _(c):
                    span = pl.ds(c * size, size)
                    twin_grad[span] = grad[pl.ds(own + c * size, size)] + twin_grad[span]
                    piece = pltpu.make_async_remote_copy(
                        src_ref=twin_grad.at[span],
                        dst_ref=out.at[span],
                        send_sem=out_send,
                        recv_sem=out_recv,
                        device_id=owner,
                        device_id_type=MESH,
                    )
                    piece.start()

                pltpu.make_async_remote_copy(
                    src_ref=twin_grad,
                    dst_ref=out,
                    send_sem=out_send,
                    recv_sem=out_recv,
                    device_id=owner,
                    device_id_type=MESH,
                ).wait()


def shards(
    count, coef, fwd_prev, fwd_now, adj_next, adj_after, encode, wavelet, shot_cells, rec_cells, records
):
    thick, across, depth = coef.shape
    steps, shots = wavelet.shape
    receivers = rec_cells.shape[0]
    layers, rows = 2 * thick, across // 2
    me = lax.axis_index("space")
    block = 8
    chunks, lines = layers // block, block * rows

    def locate(cells):
        x = cells // (across * depth) - (me // 2) * layers
        y = (cells // depth) % across - (me % 2) * rows
        inside = (x >= 0) & (x < layers) & (y >= 0) & (y < rows)
        return jnp.where(inside, x * rows + y, -1), cells % depth

    rec_line, rec_z = locate(rec_cells)
    shot_line, shot_z = locate(shot_cells)
    width = -(-shots // 128) * 128
    shot_line = jnp.pad(shot_line, (0, width - shots), constant_values=-1)
    amounts = jnp.pad((encode * wavelet).T, ((0, width - shots), (0, 128 - steps)))
    shot_z = jnp.pad(shot_z, (0, width - shots))
    observed = jnp.pad(records[0].T, ((0, 0), (0, 128 - steps)))
    band = np.zeros((depth, depth), np.float32)
    for offset in range(1, 5):
        band += scaled_weights[offset - 1] * (np.eye(depth, k=offset) + np.eye(depth, k=-offset))

    vmem = pl.BlockSpec(memory_space=pltpu.VMEM)
    hbm = pl.BlockSpec(memory_space=pl.ANY)
    return pl.pallas_call(
        functools.partial(kernel, count),
        out_shape=jax.ShapeDtypeStruct((thick, rows, depth), f32),
        in_specs=[hbm] * 5 + [vmem] * 8,
        out_specs=vmem,
        scratch_shapes=[
            pltpu.VMEM((chunks, receivers, lines), bf16),
            pltpu.VMEM((chunks, lines, receivers), bf16),
            pltpu.VMEM((chunks, lines, width), bf16),
            pltpu.VMEM((receivers, depth), f32),
            pltpu.VMEM((layers, rows, depth), f32),
            pltpu.VMEM((thick, rows, depth), f32),
            pltpu.VMEM((2, layers + 8, rows + 16, depth), f32),
            pltpu.VMEM((2, layers, rows, depth), f32),
            pltpu.VMEM((layers, rows, depth), f32),
            pltpu.VMEM((steps, layers, rows, depth), f32),
            pltpu.VMEM((receivers, depth), f32),
            pltpu.VMEM((receivers, 128), f32),
            pltpu.SemaphoreType.DMA((5,)),
            pltpu.SemaphoreType.DMA((5,)),
            pltpu.SemaphoreType.DMA((5,)),
            pltpu.SemaphoreType.DMA,
            pltpu.SemaphoreType.DMA,
            pltpu.SemaphoreType.DMA((3, 2)),
            pltpu.SemaphoreType.DMA((3, 2)),
            pltpu.SemaphoreType.DMA,
            pltpu.SemaphoreType.DMA,
            pltpu.SemaphoreType.DMA,
            pltpu.SemaphoreType.DMA,
        ],
        compiler_params=pltpu.CompilerParams(
            collective_id=0, has_side_effects=True, vmem_limit_bytes=60 * 1024 * 1024
        ),
    )(
        coef,
        fwd_prev[0],
        fwd_now[0],
        adj_next[0],
        adj_after[0],
        jnp.asarray(band, bf16),
        rec_line[None, :],
        rec_line[:, None],
        rec_z[:, None],
        shot_line[None, :],
        shot_z[:, None],
        amounts,
        observed,
    )


def solution(mesh):
    placed = (
        P(("groups", "space"), None, None),
        P(("groups", "shot"), "space", None, None),
        P(("groups", "shot"), "space", None, None),
        P(("groups", "shot"), "space", None, None),
        P(("groups", "shot"), "space", None, None),
        P(("groups", "shot"), None),
        P("groups", None),
        P("groups"),
        P("groups"),
        P(("groups", "shot"), None, None),
    )
    return jax.shard_map(
        functools.partial(shards, mesh.shape["space"]),
        mesh=mesh,
        in_specs=placed,
        out_specs=P(("groups", "space"), "shot", None),
        check_vma=False,
    )
```

```python
import functools

import jax
import jax.numpy as jnp
import numpy as np
from jax import lax
from jax.experimental import pallas as pl
from jax.experimental.pallas import tpu as pltpu
from jax.sharding import PartitionSpec as P

stencil_weights = (-205.0 / 72.0, 8.0 / 5.0, -1.0 / 5.0, 8.0 / 315.0, -1.0 / 560.0)
scaled_weights = (8064.0, -1008.0, 128.0, -9.0)
MESH = pl.DeviceIdType.MESH
f32 = jnp.float32
bf16 = jnp.bfloat16


def split(value):
    high = value.astype(bf16)
    low = (value - high.astype(f32)).astype(bf16)
    return high, low


def dot(a, b):
    return jnp.dot(a, b, preferred_element_type=f32)


def kernel(
    count,
    coef_in,
    prev_in,
    now_in,
    next_in,
    after_in,
    band,
    row_band,
    rec_line,
    rec_column,
    rec_level,
    shot_line,
    shot_level,
    shot_amounts,
    observed,
    out,
    pick,
    place,
    shot_place,
    rec_depth,
    grad,
    twin_grad,
    field,
    adj,
    coef,
    history,
    sampled,
    misfit,
    in_local,
    in_send,
    in_recv,
    twin_send,
    twin_recv,
    face_send,
    face_recv,
    half_send,
    half_recv,
    out_send,
    out_recv,
):
    steps = history.shape[0]
    layers, rows, depth = coef.shape
    half = layers // 2
    me = lax.axis_index("space")
    core = lax.axis_index("shot")
    side = lax.rem(me, 2)
    partner = me + 1 - 2 * side
    has_left = me >= 2
    has_right = me < count - 2

    for slot in range(2):
        field[slot, 0:4] = jnp.zeros((4,) + field.shape[2:], f32)
        field[slot, layers + 4 : layers + 8] = jnp.zeros((4,) + field.shape[2:], f32)

        @pl.loop(0, layers)
        def _(x):
            field[slot, x + 4, 0:8] = jnp.zeros((8, depth), f32)
            field[slot, x + 4, rows + 8 : rows + 16] = jnp.zeros((8, depth), f32)

    barrier = pltpu.get_barrier_semaphore()
    pl.semaphore_signal(barrier, inc=1, device_id={"space": partner}, device_id_type=MESH)

    pl.semaphore_signal(barrier, inc=1, device_id={"shot": 1 - core}, device_id_type=MESH)

    @pl.when(has_left)
    def _():
        pl.semaphore_signal(barrier, inc=1, device_id={"space": me - 2}, device_id_type=MESH)

    @pl.when(has_right)
    def _():
        pl.semaphore_signal(barrier, inc=1, device_id={"space": me + 2}, device_id_type=MESH)

    crossed = side != core
    owner = {"space": partner, "shot": 1 - core}

    @pl.when(crossed)
    def _():
        pl.semaphore_signal(barrier, inc=1, device_id=owner, device_id_type=MESH)

    peers = 2 + jnp.where(crossed, 1, 0) + jnp.where(has_left, 1, 0) + jnp.where(has_right, 1, 0)
    pl.semaphore_wait(barrier, peers)

    first = pl.multiple_of(side * half, half)
    keep = pl.multiple_of(side * rows, rows)
    give = pl.multiple_of(rows - side * rows, rows)
    part = half // 2
    mine = pl.multiple_of(core * part, part)
    chunk = half // 8
    targets = (
        (now_in, field.at[0, pl.ds(4 + first, half), pl.ds(8, rows)]),
        (prev_in, field.at[1, pl.ds(4 + first, half), pl.ds(8, rows)]),
        (coef_in, coef.at[pl.ds(first, half)]),
        (next_in, adj.at[0, pl.ds(first, half)]),
        (after_in, adj.at[1, pl.ds(first, half)]),
    )

    def swap(index, start, size):
        source, target = targets[index]
        return pltpu.make_async_remote_copy(
            src_ref=source.at[pl.ds(start, size), pl.ds(give, rows)],
            dst_ref=target.at[pl.ds(start, size)],
            send_sem=in_send.at[index],
            recv_sem=in_recv.at[index],
            device_id={"space": partner},
            device_id_type=MESH,
        )

    def stay(index):
        source, target = targets[index]
        return pltpu.make_async_copy(source.at[:, pl.ds(keep, rows)], target, in_local.at[index])

    def arrive(index):
        stay(index).wait()
        swap(index, 0, half).wait()

    swap(0, 0, half).start()
    swap(1, 0, half).start()
    swap(2, mine, part).start()
    for index in range(5):
        stay(index).start()

    def share():
        swap(2, mine, part).wait()
        received = coef.at[pl.ds(half - first + mine, part)]
        return pltpu.make_async_remote_copy(
            src_ref=received,
            dst_ref=received,
            send_sem=twin_send,
            recv_sem=twin_recv,
            device_id={"shot": 1 - core},
            device_id_type=MESH,
        )

    def faces(slot):
        near = (rows - 4) * (1 - side) + 8
        far = rows * side + 8 * side + 4 * (1 - side)
        inner = pl.ds(8, rows)
        to_left = pltpu.make_async_remote_copy(
            src_ref=field.at[slot, pl.ds(4, 4), inner],
            dst_ref=field.at[slot, pl.ds(layers + 4, 4), inner],
            send_sem=face_send.at[0, slot],
            recv_sem=face_recv.at[0, slot],
            device_id={"space": me - 2},
            device_id_type=MESH,
        )
        to_right = pltpu.make_async_remote_copy(
            src_ref=field.at[slot, pl.ds(layers, 4), inner],
            dst_ref=field.at[slot, pl.ds(0, 4), inner],
            send_sem=face_send.at[1, slot],
            recv_sem=face_recv.at[1, slot],
            device_id={"space": me + 2},
            device_id_type=MESH,
        )
        across = pltpu.make_async_remote_copy(
            src_ref=field.at[slot, pl.ds(4, layers), pl.ds(near, 4)],
            dst_ref=field.at[slot, pl.ds(4, layers), pl.ds(far, 4)],
            send_sem=face_send.at[2, slot],
            recv_sem=face_recv.at[2, slot],
            device_id={"space": partner},
            device_id_type=MESH,
        )
        return to_left, to_right, across

    def send_faces(slot):
        to_left, to_right, across = faces(slot)
        pl.when(has_left)(to_left.start)
        pl.when(has_right)(to_right.start)
        across.start()

    def receive_faces(slot):
        to_left, to_right, across = faces(slot)

        @pl.when(has_left)
        def _():
            to_left.wait_send()
            to_right.wait_recv()

        @pl.when(has_right)
        def _():
            to_right.wait_send()
            to_left.wait_recv()

        across.wait()

    block = 8
    lines = block * rows

    def flat(value):
        return value.reshape(lines, depth)

    def store_sample(step):
        value = jnp.sum(sampled[...] * rec_depth[...], axis=1, keepdims=True)
        lane = lax.broadcasted_iota(jnp.int32, misfit.shape, 1)
        misfit[...] = jnp.where(lane == step, value, misfit[...])

    def add_sample(c, high, low):
        chooser = pick[c]
        found = dot(chooser, high) + dot(chooser, low)

        @pl.when(c == 0)
        def _():
            sampled[...] = found

        @pl.when(c > 0)
        def _():
            sampled[...] += found

    def depthwise(value, high, low):
        along = dot(high, band[...]) + dot(low, band[...])
        return along.reshape(value.shape) * (1.0 / 5040.0) + (3.0 * stencil_weights[0]) * value

    def add_sides(slot, x, low, tall, total):
        wide = field[slot, 4 + x, pl.ds(low, tall + 16)]
        here = pl.ds(pl.multiple_of(low + 8, 8), tall)
        high, rest = split(wide)
        mixer = row_band[0:tall, 0 : tall + 16].astype(bf16)
        total = total + (dot(mixer, high) + dot(mixer, rest)) * (1.0 / 5040.0)
        for offset in range(1, 5):
            pair = field[slot, 4 + x + offset, here] + field[slot, 4 + x - offset, here]
            total = total + stencil_weights[offset] * pair
        return total

    inner_low = pl.multiple_of(8 * side, 8)
    edge_low = pl.multiple_of((rows - 8) * (1 - side), 8)

    def rim(unit):
        @pl.loop(0, 4)
        def _(x):
            unit(x, 0, rows)
            unit(layers - 4 + x, 0, rows)

        @pl.loop(1, layers // 4 - 1)
        def _(x):
            for inside in range(4):
                unit(4 * x + inside, edge_low, 8)

    def interior(unit):
        @pl.loop(2, layers // 2 - 2)
        def _(x):
            unit(2 * x, inner_low, rows - 8)
            unit(2 * x + 1, inner_low, rows - 8)

    misfit[...] = jnp.zeros_like(misfit)

    def one_hot(index, shape, axis, start, kind):
        hit = lax.broadcasted_iota(jnp.int32, shape, axis) + start == index
        return jnp.where(hit, 1.0, 0.0).astype(kind)

    receivers, shots_held = rec_depth.shape[0], shot_place.shape[2]
    rec_depth[...] = one_hot(rec_level[...], rec_depth.shape, 1, 0, f32)

    @pl.loop(0, layers // block)
    def _(c):
        start = c * lines
        pick[c] = one_hot(rec_column[...], (receivers, lines), 1, start, bf16)
        place[c] = one_hot(rec_line[...], (lines, receivers), 0, start, bf16)
        shot_place[c] = one_hot(shot_line[...], (lines, shots_held), 0, start, bf16)

    arrive(0)
    send_faces(0)
    arrive(1)

    @pl.loop(0, steps)
    def _(step):
        slot = lax.rem(step, 2)
        other = 1 - slot
        shot_lane = lax.broadcasted_iota(jnp.int32, shot_amounts.shape, 1)
        shot_amount = jnp.sum(jnp.where(shot_lane == step, shot_amounts[...], 0.0), axis=1, keepdims=True)
        shot_depth = one_hot(shot_level[...], (shots_held, depth), 1, 0, f32)
        amount_high, amount_low = split(shot_amount * shot_depth)

        @pl.when(step < 8)
        def _():
            swap(3, step * chunk, chunk).start()
            swap(4, step * chunk, chunk).start()

        @pl.loop(0, layers // block)
        def _(c):
            span = pl.ds(c * block, block)
            mid = pl.ds(4 + c * block, block)
            value = field[slot, mid, 8 : rows + 8, :]
            high, low = split(flat(value))
            history[step, span] = depthwise(value, high, low)
            spots = shot_place[c]
            shots = dot(spots, amount_high) + dot(spots, amount_low)
            before = field[other, mid, 8 : rows + 8, :]
            field[other, mid, 8 : rows + 8, :] = 2.0 * value - before + shots.reshape(value.shape)
            add_sample(c, high, low)

        store_sample(step - 1)

        @pl.when(step == 0)
        def _():
            stay(2).wait()
            passed = share()
            passed.start()
            passed.wait()

        receive_faces(slot)

        def unit(x, low, tall):
            mine = pl.ds(low, tall)
            total = add_sides(slot, x, low, tall, history[step, x, mine])
            history[step, x, mine] = total
            field[other, 4 + x, pl.ds(pl.multiple_of(low + 8, 8), tall)] += coef[x, mine] * total

        rim(unit)

        @pl.when(step < steps - 1)
        def _():
            send_faces(other)

        interior(unit)

    last = steps % 2

    @pl.loop(0, layers // block)
    def _(c):
        add_sample(c, *split(flat(field[last, pl.ds(4 + c * block, block), 8 : rows + 8, :])))

    store_sample(steps - 1)
    misfit[...] = misfit[...] - observed[...]
    arrive(3)
    arrive(4)

    @pl.loop(0, layers)
    def _(x):
        field[last, 4 + x, 8 : rows + 8] = coef[x] * adj[0, x]
        grad[x] = jnp.zeros((rows, depth), f32)

    send_faces(last)

    @pl.loop(0, steps)
    def _(back):
        slot = lax.rem(back + steps, 2)
        other = 1 - slot
        later = lax.rem(back, 2)
        latest = 1 - later
        step = steps - 1 - back
        lane = lax.broadcasted_iota(jnp.int32, misfit.shape, 1)
        amount = jnp.sum(jnp.where(lane == step, misfit[...], 0.0), axis=1, keepdims=True)
        amount_high, amount_low = split(amount * rec_depth[...])

        @pl.loop(0, layers // block)
        def _(c):
            span = pl.ds(c * block, block)
            value = field[slot, pl.ds(4 + c * block, block), 8 : rows + 8, :]
            spots = place[c]
            added = dot(spots, amount_high) + dot(spots, amount_low)
            adj[latest, span] = (
                2.0 * adj[later, span]
                - adj[latest, span]
                + depthwise(value, *split(flat(value)))
                + added.reshape(value.shape)
            )

        receive_faces(slot)

        def unit(x, low, tall):
            mine = pl.ds(low, tall)
            total = add_sides(slot, x, low, tall, adj[latest, x, mine])
            adj[latest, x, mine] = total
            field[other, 4 + x, pl.ds(pl.multiple_of(low + 8, 8), tall)] = coef[x, mine] * total
            grad[x, mine] += total * history[step, x, mine]

        @pl.when(back < steps - 1)
        def _():
            rim(unit)
            send_faces(other)
            interior(unit)

        @pl.when(back == steps - 1)
        def _():
            own = pl.multiple_of(core * half, half)
            handed = half - own

            @pl.loop(0, half)
            def _(x):
                unit(handed + x, 0, rows)

            halves = pltpu.make_async_remote_copy(
                src_ref=grad.at[pl.ds(handed, half)],
                dst_ref=twin_grad,
                send_sem=half_send,
                recv_sem=half_recv,
                device_id={"shot": 1 - core},
                device_id_type=MESH,
            )
            halves.start()

            @pl.loop(0, half)
            def _(x):
                unit(own + x, 0, rows)

            halves.wait()

            @pl.when(jnp.logical_not(crossed))
            def _():
                @pl.loop(0, half)
                def _(x):
                    out[x] = grad[own + x] + twin_grad[x]

            @pl.when(crossed)
            def _():
                size = half // 4

                @pl.loop(0, 4)
                def _(c):
                    span = pl.ds(c * size, size)
                    twin_grad[span] = grad[pl.ds(own + c * size, size)] + twin_grad[span]
                    piece = pltpu.make_async_remote_copy(
                        src_ref=twin_grad.at[span],
                        dst_ref=out.at[span],
                        send_sem=out_send,
                        recv_sem=out_recv,
                        device_id=owner,
                        device_id_type=MESH,
                    )
                    piece.start()

                pltpu.make_async_remote_copy(
                    src_ref=twin_grad,
                    dst_ref=out,
                    send_sem=out_send,
                    recv_sem=out_recv,
                    device_id=owner,
                    device_id_type=MESH,
                ).wait()


def shards(
    count, coef, fwd_prev, fwd_now, adj_next, adj_after, encode, wavelet, shot_cells, rec_cells, records
):
    thick, across, depth = coef.shape
    steps, shots = wavelet.shape
    receivers = rec_cells.shape[0]
    layers, rows = 2 * thick, across // 2
    me = lax.axis_index("space")
    block = 8
    chunks, lines = layers // block, block * rows

    def locate(cells):
        x = cells // (across * depth) - (me // 2) * layers
        y = (cells // depth) % across - (me % 2) * rows
        inside = (x >= 0) & (x < layers) & (y >= 0) & (y < rows)
        return jnp.where(inside, x * rows + y, -1), cells % depth

    rec_line, rec_z = locate(rec_cells)
    shot_line, shot_z = locate(shot_cells)
    width = -(-shots // 128) * 128
    shot_line = jnp.pad(shot_line, (0, width - shots), constant_values=-1)
    amounts = jnp.pad((encode * wavelet).T, ((0, width - shots), (0, 128 - steps)))
    shot_z = jnp.pad(shot_z, (0, width - shots))
    observed = jnp.pad(records[0].T, ((0, 0), (0, 128 - steps)))
    band = np.zeros((depth, depth), np.float32)
    for offset in range(1, 5):
        band += scaled_weights[offset - 1] * (np.eye(depth, k=offset) + np.eye(depth, k=-offset))

    row_band = np.zeros((rows, rows + 16), np.float32)
    for offset in range(1, 5):
        for shift in (offset, -offset):
            row_band += scaled_weights[offset - 1] * np.eye(rows, rows + 16, k=8 + shift)

    vmem = pl.BlockSpec(memory_space=pltpu.VMEM)
    hbm = pl.BlockSpec(memory_space=pl.ANY)
    return pl.pallas_call(
        functools.partial(kernel, count),
        out_shape=jax.ShapeDtypeStruct((thick, rows, depth), f32),
        in_specs=[hbm] * 5 + [vmem] * 9,
        out_specs=vmem,
        scratch_shapes=[
            pltpu.VMEM((chunks, receivers, lines), bf16),
            pltpu.VMEM((chunks, lines, receivers), bf16),
            pltpu.VMEM((chunks, lines, width), bf16),
            pltpu.VMEM((receivers, depth), f32),
            pltpu.VMEM((layers, rows, depth), f32),
            pltpu.VMEM((thick, rows, depth), f32),
            pltpu.VMEM((2, layers + 8, rows + 16, depth), f32),
            pltpu.VMEM((2, layers, rows, depth), f32),
            pltpu.VMEM((layers, rows, depth), f32),
            pltpu.VMEM((steps, layers, rows, depth), f32),
            pltpu.VMEM((receivers, depth), f32),
            pltpu.VMEM((receivers, 128), f32),
            pltpu.SemaphoreType.DMA((5,)),
            pltpu.SemaphoreType.DMA((5,)),
            pltpu.SemaphoreType.DMA((5,)),
            pltpu.SemaphoreType.DMA,
            pltpu.SemaphoreType.DMA,
            pltpu.SemaphoreType.DMA((3, 2)),
            pltpu.SemaphoreType.DMA((3, 2)),
            pltpu.SemaphoreType.DMA,
            pltpu.SemaphoreType.DMA,
            pltpu.SemaphoreType.DMA,
            pltpu.SemaphoreType.DMA,
        ],
        compiler_params=pltpu.CompilerParams(
            collective_id=0, has_side_effects=True, vmem_limit_bytes=60 * 1024 * 1024
        ),
    )(
        coef,
        fwd_prev[0],
        fwd_now[0],
        adj_next[0],
        adj_after[0],
        jnp.asarray(band, bf16),
        jnp.asarray(row_band, f32),
        rec_line[None, :],
        rec_line[:, None],
        rec_z[:, None],
        shot_line[None, :],
        shot_z[:, None],
        amounts,
        observed,
    )


def solution(mesh):
    placed = (
        P(("groups", "space"), None, None),
        P(("groups", "shot"), "space", None, None),
        P(("groups", "shot"), "space", None, None),
        P(("groups", "shot"), "space", None, None),
        P(("groups", "shot"), "space", None, None),
        P(("groups", "shot"), None),
        P("groups", None),
        P("groups"),
        P("groups"),
        P(("groups", "shot"), None, None),
    )
    return jax.shard_map(
        functools.partial(shards, mesh.shape["space"]),
        mesh=mesh,
        in_specs=placed,
        out_specs=P(("groups", "space"), "shot", None),
        check_vma=False,
    )
```
